512 devices in a mesh: pipe: 32 (over y_hi, z), tensor: 8 (over y_lo, x), dp: 2 (over core).
Axes of the slice: x: 4, y: 8 (y_hi: 4, y_lo: 2; y = y_hi * 2 + y_lo), z: 8, core: 2. Of those that a mesh axis runs over, the one named last changes fastest.
Arguments:
- fwd_in: bfloat16 [32, 512, 4096], P('pipe', 'dp', 'tensor'), may hold values from -6 to 6
- parked: bfloat16 [32, 512, 4096], P('pipe', 'dp', 'tensor'), may hold values from -6 to 6
- grad_in: bfloat16 [32, 512, 4096], P('pipe', 'dp', 'tensor'), may hold values from -6 to 6
- positions: int32 [32, 2, 2], P('pipe', 'dp'), may hold values from 0 to 768, as said below
- kv_cache: bfloat16 [32, 2, 2, 512, 256], P('pipe', 'dp'), may hold values from -6 to 6
- w_query: bfloat16 [32, 4096, 1024], P('pipe', 'tensor', 'dp'), may hold values from -0.09375 to 0.09375
- w_keyval: bfloat16 [32, 4096, 256], P('pipe', 'tensor'), may hold values from -0.09375 to 0.09375
- w_out: bfloat16 [32, 1024, 4096], P('pipe', 'tensor', 'dp'), may hold values from -0.1875 to 0.1875
- gain: bfloat16 [32, 4096], P('pipe', 'tensor'), may hold values from 0.5 to 1.5
Outputs:
- next_act: bfloat16 [32, 512, 4096], P('pipe', 'dp', 'tensor')
- prev_grad: bfloat16 [32, 512, 4096], P('pipe', 'dp', 'tensor')
- grad_query: bfloat16 [32, 4096, 1024], P('pipe', 'tensor', 'dp')
- grad_keyval: float32 [32, 4096, 256], P('pipe', 'tensor')
- grad_out: bfloat16 [32, 1024, 4096], P('pipe', 'tensor', 'dp')
- grad_gain: float32 [32, 4096], P('pipe', 'tensor')
The draws below stay inside these ranges and needn't reach their ends.
Inputs may be any that keep to these rules, and one draw needn't show every extreme that they name: `positions`: each is a multiple of 256.
All inputs are finite; a program needn't handle non-finite values.
Results may differ from the reference program's by a relative error of at most 0.028.
Values may be sent and summed in bfloat16 or wider, within the bound.
A program may use at most 64 MiB of HBM per device.

```python
import math
import jax
import jax.numpy as jnp
from jax import lax

D = 4096
HEAD = 128
GROUP = 8
TOK_DEV = 256
CTX = 512
ROWS = 512
N_PIPE = 32
N_TENSOR = 8
N_DP = 2


def draw_positions(key, part):
    key = jax.random.fold_in(key, 7)
    return TOK_DEV * jax.random.randint(key, (N_PIPE, N_DP, 2), 0, 4, dtype=jnp.int32)


def block_scale(stream_key, dims, pieces, low, high):
    def one(dim, shards_of):
        steps = jax.random.uniform(jax.random.fold_in(jax.random.fold_in(stream_key, 6), dim), (shards_of,), jnp.float32, low / len(pieces), high / len(pieces))
        return jnp.repeat(jnp.exp(steps), dims[dim] // shards_of).reshape((-1,) + (1,) * (len(dims) - dim - 1))

    level = one(*pieces[0])
    for cut in pieces[1:]:
        level = level * one(*cut)
    return level


def normal_values(rng, shape, spread, bound, pieces=(), kind=jnp.bfloat16):
    values = jax.random.normal(rng, shape, jnp.float32) * spread
    if len(pieces) > 0:
        values = block_scale(rng, shape, pieces, -0.22, 0.18) * values
    return jnp.clip(values, min=-bound, max=bound).astype(kind)


def setup_inputs(seed: int = 0) -> dict:
    arg_keys = jax.random.split(jax.random.key(seed), 10)
    fwd_in = normal_values(arg_keys[0], (N_PIPE, ROWS, D), 1.0, 6.0, ((0, 32), (1, 2), (2, 8)))
    parked = normal_values(arg_keys[1], (N_PIPE, ROWS, D), 1.0, 6.0, ((0, 32), (1, 2), (2, 8)))
    grad_in = normal_values(arg_keys[2], (N_PIPE, ROWS, D), 1.0, 6.0, ((0, 32), (1, 2), (2, 8)))
    positions = draw_positions(jax.random.fold_in(arg_keys[9], 71), 0)
    kv_cache = normal_values(arg_keys[4], (N_PIPE, N_DP, 2, CTX, 2 * HEAD), 1.0, 6.0, ((0, 32), (1, 2)))
    w_query = normal_values(arg_keys[5], (N_PIPE, D, GROUP * HEAD), D ** -0.5, 0.09375, ((0, 32), (1, 8), (2, 2)))
    w_keyval = normal_values(arg_keys[6], (N_PIPE, D, 2 * HEAD), D ** -0.5, 0.09375, ((0, 32), (1, 8)))
    w_out = normal_values(arg_keys[7], (N_PIPE, GROUP * HEAD, D), (GROUP * HEAD) ** -0.5, 0.1875, ((0, 32), (1, 8), (2, 2)))
    gain = jnp.clip(1.0 + 0.1 * jax.random.normal(arg_keys[8], (N_PIPE, D), jnp.float32), 0.5, 1.5).astype(jnp.bfloat16)
    return dict(fwd_in=fwd_in, parked=parked, grad_in=grad_in, positions=positions, kv_cache=kv_cache, w_query=w_query, w_keyval=w_keyval, w_out=w_out, gain=gain)


eps = 1e-05

def visible(rows, span, start):
    column = jnp.arange(span + rows, dtype=jnp.int32)[None, :]
    line = jnp.arange(rows, dtype=jnp.int32)[:, None]
    live = jnp.minimum(start, span).astype(jnp.int32)
    return jnp.where(column < span, column >= span - live, column - span <= line)

def attend(query, keyval, cache, start, heads):
    rows = query.shape[0]
    span = cache.shape[0]
    size = keyval.shape[1] // 2
    keys = jnp.concatenate([cache[:, :size], keyval[:, :size]], axis=0).astype(jnp.float32)
    values = jnp.concatenate([cache[:, size:], keyval[:, size:]], axis=0).astype(jnp.float32)
    query_heads = query.reshape(rows, heads, size).astype(jnp.float32)
    scores = jnp.einsum('rhd,kd->hrk', query_heads, keys) / math.sqrt(size)
    scores = jnp.where(visible(rows, span, start)[None], scores, -1e+30)
    weights = jax.nn.softmax(scores, axis=-1)
    probs = weights.astype(jnp.bfloat16)
    mixed = jnp.einsum('hrk,kd->rhd', probs.astype(jnp.float32), values)
    return (mixed.reshape(rows, heads * size).astype(jnp.bfloat16), weights, probs, keys, values, query_heads)

def attend_back(grad_mixed, weights, probs, keys, values, query_heads, span):
    rows, heads, size = query_heads.shape
    grad_heads = grad_mixed.reshape(rows, heads, size).astype(jnp.float32)
    grad_probs = jnp.einsum('rhd,kd->hrk', grad_heads, values)
    grad_scores = weights * (grad_probs - lax.optimization_barrier(jnp.sum(grad_probs * weights, axis=-1, keepdims=True))) / math.sqrt(size)
    scores_low = grad_scores.astype(jnp.bfloat16).astype(jnp.float32)
    grad_query = jnp.einsum('hrk,kd->rhd', scores_low, keys).reshape(rows, heads * size)
    grad_keys = jnp.einsum('hrk,rhd->kd', scores_low[:, :, span:], query_heads)
    grad_values = jnp.einsum('hrk,rhd->kd', probs[:, :, span:].astype(jnp.float32), grad_heads)
    return (grad_query, jnp.concatenate([grad_keys, grad_values], axis=1))

def normalize(x, gain_row):
    xf = x.astype(jnp.float32)
    scale = lax.rsqrt(lax.optimization_barrier(jnp.mean(xf * xf, axis=1)) + eps)
    normed = (xf * scale[:, None] * gain_row.astype(jnp.float32)).astype(jnp.bfloat16)
    return (xf, scale, normed)

def head_sum(mixed, w_out):
    rows = mixed.shape[0]
    groups = N_TENSOR
    parted = mixed.reshape(rows, groups, -1).astype(jnp.float32)
    weights = w_out.reshape(groups, parted.shape[2], -1).astype(jnp.float32)
    parts = jnp.einsum('rgc,gcd->grd', parted, weights).astype(jnp.bfloat16).astype(jnp.float32)
    return lax.optimization_barrier(jnp.sum(parts, axis=0))

def section_pass(x, saved, grad, start_fwd, start_bwd, cache_fwd, cache_bwd, gain_row, w_query, w_keyval, w_out):
    xf, scale, normed = normalize(x, gain_row)
    query = jnp.dot(normed, w_query, preferred_element_type=jnp.float32).astype(jnp.bfloat16)
    keyval = jnp.dot(normed, w_keyval, preferred_element_type=jnp.float32).astype(jnp.bfloat16)
    mixed = attend(query, keyval, cache_fwd, start_fwd, GROUP)[0]
    result = (xf + head_sum(mixed, w_out)).astype(jnp.bfloat16)
    saved_f, saved_scale, saved_normed = normalize(saved, gain_row)
    saved_query = jnp.dot(saved_normed, w_query, preferred_element_type=jnp.float32).astype(jnp.bfloat16)
    saved_keyval = jnp.dot(saved_normed, w_keyval, preferred_element_type=jnp.float32).astype(jnp.bfloat16)
    mixed_b, weights, probs, keys, values, query_heads = attend(saved_query, saved_keyval, cache_bwd, start_bwd, GROUP)
    grad_wout = jnp.dot(mixed_b.T, grad, preferred_element_type=jnp.float32)
    grad_mixed = jnp.dot(grad, w_out.T, preferred_element_type=jnp.float32).astype(jnp.bfloat16)
    grad_q, grad_kv = attend_back(grad_mixed, weights, probs, keys, values, query_heads, cache_bwd.shape[0])
    grad_q = grad_q.astype(jnp.bfloat16)
    grad_kv = grad_kv.astype(jnp.bfloat16)
    grad_wq = jnp.dot(saved_normed.T, grad_q, preferred_element_type=jnp.float32)
    grad_wkv = jnp.dot(saved_normed.T, grad_kv, preferred_element_type=jnp.float32)
    grad_normed = jnp.dot(grad_q, w_query.T, preferred_element_type=jnp.float32) + jnp.dot(grad_kv, w_keyval.T, preferred_element_type=jnp.float32)
    gain_f = gain_row.astype(jnp.float32)
    grad_gain = lax.optimization_barrier(jnp.sum(grad_normed * saved_f * saved_scale[:, None], axis=0))
    grad_x = grad.astype(jnp.float32) + grad_normed * gain_f * saved_scale[:, None]
    return (result, grad_x.astype(jnp.bfloat16), grad_wq, grad_wkv, grad_wout, grad_gain)

def reference(fwd_in, parked, grad_in, positions, kv_cache, w_query, w_keyval, w_out, gain):
    rows = TOK_DEV
    acts = fwd_in.reshape(N_PIPE, N_DP, rows, -1)
    saved_all = parked.reshape(N_PIPE, N_DP, rows, -1)
    grads = grad_in.reshape(N_PIPE, N_DP, rows, -1)

    def per_section(section):
        results = []
        partner = (N_PIPE - 1 - section).astype(jnp.int32)
        for replica in range(N_DP):
            results.append(section_pass(acts[section, replica], saved_all[partner, replica], grads[section, replica], positions[section, replica, 0], positions[section, replica, 1], kv_cache[section, replica, 0], kv_cache[section, replica, 1], gain[section], w_query[section], w_keyval[section], w_out[section]))
        outs = jnp.stack([item[0] for item in results])
        back = jnp.stack([item[1] for item in results])
        sum_q = sum((item[2].astype(jnp.bfloat16).astype(jnp.float32) for item in results)).astype(jnp.bfloat16)
        sum_kv = sum((item[3] for item in results))
        sum_o = sum((item[4].astype(jnp.bfloat16).astype(jnp.float32) for item in results)).astype(jnp.bfloat16)
        sum_gain = sum((item[5] for item in results))
        return (outs, back, sum_q, sum_kv, sum_o, sum_gain)
    outs, back, sum_q, sum_kv, sum_o, sum_gain = lax.map(per_section, jnp.arange(N_PIPE, dtype=jnp.int32))
    zero_block = jnp.zeros_like(outs[:1])
    next_act = jnp.concatenate([zero_block, outs[:-1]], axis=0).reshape(N_PIPE, N_DP * rows, -1)
    prev_grad = jnp.concatenate([back[1:], zero_block], axis=0).reshape(N_PIPE, N_DP * rows, -1)
    return (next_act, prev_grad, sum_q, sum_kv, sum_o, sum_gain)
```

```python
import functools
import math

import jax
import jax.numpy as jnp
from jax import lax
from jax.experimental import pallas as pl
from jax.experimental.pallas import tpu as pltpu
from jax.sharding import PartitionSpec as P

HEAD = 128
MESH = pl.DeviceIdType.MESH
eps = 1e-05
BF = jnp.bfloat16
F32 = jnp.float32


def mm(a, b):
    return lax.dot_general(a, b, (((1,), (0,)), ((), ())), preferred_element_type=F32)


def mm_bt(a, b):
    return lax.dot_general(a, b, (((1,), (1,)), ((), ())), preferred_element_type=F32)


def mm_at(a, b):
    return lax.dot_general(a, b, (((0,), (0,)), ((), ())), preferred_element_type=F32)


def drain(ref, sem):
    pltpu.make_async_copy(ref, ref, sem).wait()


def side_by_side(ref, first, count):
    return jnp.concatenate([ref[first + i] for i in range(count)], axis=1)


def softmax_parts(q, kc, ko, live):
    rows, span = q.shape[0], kc.shape[0]
    factor = 1.0 / math.sqrt(HEAD)
    sc = mm_bt(q, kc) * factor
    so = mm_bt(q, ko) * factor
    col = lax.broadcasted_iota(jnp.int32, sc.shape, 1)
    sc = jnp.where(col >= span - live, sc, -1e30)
    col = lax.broadcasted_iota(jnp.int32, so.shape, 1)
    line = lax.broadcasted_iota(jnp.int32, so.shape, 0)
    so = jnp.where(col <= line, so, -1e30)
    top = jnp.maximum(jnp.max(sc, axis=1, keepdims=True), jnp.max(so, axis=1, keepdims=True))
    ec, eo = jnp.exp(sc - top), jnp.exp(so - top)
    total = jnp.sum(ec, axis=1, keepdims=True) + jnp.sum(eo, axis=1, keepdims=True)
    inverse = 1.0 / total
    return ec * inverse, eo * inverse


def kernel(
    n_pipe,
    width,
    pos, gain_ref, x_hbm, parked_hbm, grad_hbm, cache_hbm, wq_hbm, wkv_hbm, wo_hbm,
    next_out, prev_out, gwq_out, gwkv_out, gwo_out, gain_out,
    x, saved, gr, cache, wq, wkv, wot,
    qs_f, qr_f, qs_b, qr_b, ks_f, kr_f, ks_b, kr_b, ss_f, sr_f, ss_b, sr_b,
    kv_f, kv_b, scale_f, scale_b, gms, gmr, mix_f, mixb_own, mixb,
    gks, gkr, gkv, gq, gq_sib, gkv_sib, nb, nb_sib,
    y, gx, zero, wog, gwq, gwkv, gn, gn_sib,
    local_sem, wot_sem, sem_s, sem_r,
):
    s, t, d = lax.axis_index("pipe"), lax.axis_index("tensor"), lax.axis_index("dp")
    sib = 1 - d
    home = t // 4
    nt = 8
    rows = x.shape[0]
    sub = rows // nt

    barrier = pltpu.get_barrier_semaphore()
    for k in range(1, nt):
        other = lax.rem(t + k, nt)
        pl.semaphore_signal(barrier, inc=1, device_id={"tensor": other}, device_id_type=MESH)
        pl.semaphore_signal(
            barrier, inc=1, device_id={"tensor": other, "dp": sib}, device_id_type=MESH
        )
    pl.semaphore_signal(barrier, inc=1, device_id={"dp": sib}, device_id_type=MESH)
    mirror = n_pipe - 1 - s
    for stage in (mirror, lax.rem(s + 1, n_pipe), lax.rem(s + n_pipe - 1, n_pipe)):
        pl.semaphore_signal(barrier, inc=1, device_id={"pipe": stage}, device_id_type=MESH)

    loads = [
        pltpu.make_async_copy(x_hbm, x, local_sem.at[0]),
        pltpu.make_async_copy(wq_hbm, wq.at[d], local_sem.at[1]),
        pltpu.make_async_copy(wkv_hbm, wkv, local_sem.at[2]),
        pltpu.make_async_copy(grad_hbm, gr.at[d], local_sem.at[3]),
        pltpu.make_async_copy(cache_hbm, cache, local_sem.at[4]),
    ]
    for load in loads:
        load.start()
    gain = gain_ref[...].astype(F32)
    zero[...] = jnp.zeros_like(zero)

    pl.semaphore_wait(barrier, 2 * (nt - 1) + 1 + 3)

    def send(src, dst, index, device, rsem=None):
        copy = pltpu.make_async_remote_copy(
            src_ref=src,
            dst_ref=dst,
            send_sem=sem_s.at[index],
            recv_sem=sem_r.at[index] if rsem is None else rsem,
            device_id=device,
            device_id_type=MESH,
        )
        copy.start()

    def got(ref, index):
        drain(ref, sem_r.at[index])

    def sent(ref, index):
        drain(ref, sem_s.at[index])

    MIRROR, WQ, WOT, GRAD, QF, KF, SF, QB, KB, SB, KVF, KVB, GM, MIXF, MIXB, GK, GKV, GQ = range(18)
    GQS, GKVS, NB, GN, NEXT, PREV, WOG, FWD = range(18, 26)

    send(parked_hbm, saved, MIRROR, {"pipe": mirror})
    send(wq_hbm, wq.at[d], WQ, {"dp": sib})
    part = wo_hbm.shape[1] // 4
    for j in range(4):
        target = 4 * d + j
        block = wo_hbm.at[:, pl.ds(j * part, part)]

        @pl.when(target != t)
        def _():
            send(block, wot.at[t], WOT, {"tensor": target}, wot_sem.at[t])

        @pl.when(target == t)
        def _():
            pltpu.make_async_copy(block, wot.at[t], wot_sem.at[t]).start()

    send(grad_hbm, gr.at[d], GRAD, {"dp": sib})

    def to_peers(src_of, dst, index):
        for k in range(1, nt):
            other = lax.rem(t + k, nt)
            send(src_of(other), dst.at[t], index, {"tensor": other})

    def project(data, qs, qr, ks, kr, ss, sr, first):
        xf = data.astype(F32)
        xg = (xf * gain).astype(BF)
        for half in range(2):
            value = mm(xg, wq[half])
            for i in range(4):
                qs[4 * half + i] = value[:, i * HEAD : (i + 1) * HEAD].astype(BF)
        value = mm(xg, wkv[...]).astype(BF)
        for i in range(nt):
            ks[i] = value[i * sub : (i + 1) * sub]
        to_peers(lambda o: qs.at[o], qr, first)
        to_peers(lambda o: ks.at[o], kr, first + 1)
        sq = xf * xf
        quarter = sq[:, :HEAD]
        for i in range(1, sq.shape[1] // HEAD):
            quarter = quarter + sq[:, i * HEAD : (i + 1) * HEAD]
        row = jnp.sum(quarter.T, axis=0, keepdims=True)
        ss[...] = jnp.broadcast_to(row, ss.shape)
        to_peers(lambda o: ss, sr, first + 2)
        qr[t] = qs[t]
        kr[t] = ks[t]
        sr[t] = ss[...]

    def combine(qr, kr, sr, kv, scale, first, kv_index):
        got(sr.at[pl.ds(0, nt - 1)], first + 2)
        row = sr[0][0:1]
        for i in range(1, nt):
            row = row + sr[i][0:1]
        row = lax.rsqrt(row / width + eps)
        scale[...] = jnp.broadcast_to(row, (HEAD, rows)).T
        got(kr.at[pl.ds(0, nt - 1)], first + 1)
        mine = kr[0].astype(F32)
        for i in range(1, nt):
            mine = mine + kr[i].astype(F32)
        part_scale = scale[pl.ds(pl.multiple_of(t * sub, sub), sub), :]
        kv[t] = (mine * jnp.concatenate([part_scale, part_scale], axis=1)).astype(BF)
        to_peers(lambda o: kv.at[t], kv, kv_index)
        got(qr.at[pl.ds(0, nt - 1)], first)
        q = qr[0].astype(F32)
        for i in range(1, nt):
            q = q + qr[i].astype(F32)
        return (q * scale[...]).astype(BF)

    loads[0].wait()
    loads[1].wait()
    loads[2].wait()
    got(wq.at[0], WQ)
    project(x[...], qs_f, qr_f, ks_f, kr_f, ss_f, sr_f, QF)

    got(saved, MIRROR)
    project(saved[...], qs_b, qr_b, ks_b, kr_b, ss_b, sr_b, QB)

    loads[3].wait()
    for h in range(nt):
        drain(wot.at[h], wot_sem.at[h])

        @pl.when(home == d)
        def _():
            send(wot.at[h], wot.at[h], FWD, {"dp": sib}, wot_sem.at[h])

    grad = gr[d]
    for h in range(nt):
        gms[h] = mm_bt(grad, wot[h]).astype(BF)
    to_peers(lambda o: gms.at[o], gmr, GM)
    gmr[t] = gms[t]

    q_f = combine(qr_f, kr_f, sr_f, kv_f, scale_f, QF, KVF)
    q_b = combine(qr_b, kr_b, sr_b, kv_b, scale_b, QB, KVB)

    loads[4].wait()
    got(kv_f.at[pl.ds(0, nt - 1)], KVF)
    span = cache.shape[1]
    own = kv_f[...].reshape(rows, 2 * HEAD)
    live = jnp.minimum(pos[0], span)
    wc, wo_ = softmax_parts(q_f, cache[0, :, :HEAD], own[:, :HEAD], live)
    mixed = mm(wc.astype(BF), cache[0, :, HEAD:]) + mm(wo_.astype(BF), own[:, HEAD:])
    mix_f[t] = mixed.astype(BF)
    to_peers(lambda o: mix_f.at[t], mix_f, MIXF)

    got(kv_b.at[pl.ds(0, nt - 1)], KVB)
    own = kv_b[...].reshape(rows, 2 * HEAD)
    live = jnp.minimum(pos[1], span)
    kc, vc, ko, vo = cache[1, :, :HEAD], cache[1, :, HEAD:], own[:, :HEAD], own[:, HEAD:]
    wc, wo_ = softmax_parts(q_b, kc, ko, live)
    pc, po = wc.astype(BF), wo_.astype(BF)
    mixb_own[...] = (mm(pc, vc) + mm(po, vo)).astype(BF)
    seat = lax.rem(t, 4)
    for k in range(nt):
        other = lax.rem(t + k, nt)
        if k == 0:

            @pl.when(home != d)
            def _():
                send(mixb_own, mixb.at[d, seat], MIXB, {"dp": sib})

            @pl.when(home == d)
            def _():
                pltpu.make_async_copy(mixb_own, mixb.at[d, seat], sem_r.at[MIXB]).start()

        else:
            send(mixb_own, mixb.at[d, seat], MIXB, {"tensor": other, "dp": home})

    got(gmr.at[pl.ds(0, nt - 1)], GM)
    gm = gmr[0].astype(F32)
    for i in range(1, nt):
        gm = gm + gmr[i].astype(F32)
    gm = gm.astype(BF)
    gpc, gpo = mm_bt(gm, vc), mm_bt(gm, vo)
    mean = jnp.sum(gpc * wc, axis=1, keepdims=True) + jnp.sum(gpo * wo_, axis=1, keepdims=True)
    factor = 1.0 / math.sqrt(HEAD)
    gsc = (wc * (gpc - mean) * factor).astype(BF)
    gso = (wo_ * (gpo - mean) * factor).astype(BF)
    gkeys = mm_at(gso, q_b).astype(BF)
    gvals = mm_at(po, gm).astype(BF)
    for i in range(nt):
        gks[i, :, :HEAD] = gkeys[i * sub : (i + 1) * sub]
        gks[i, :, HEAD:] = gvals[i * sub : (i + 1) * sub]
    to_peers(lambda o: gks.at[o], gkr, GK)
    gkr[t] = gks[t]
    gq[t] = (mm(gsc, kc) + mm(gso, ko)).astype(BF)
    to_peers(lambda o: gq.at[t], gq, GQ)

    saved_f = saved[...].astype(F32)
    wide = jnp.concatenate([scale_b[...]] * (saved.shape[1] // HEAD), axis=1)
    nb[...] = (saved_f * wide * gain).astype(BF)
    send(nb, nb_sib, NB, {"dp": sib})

    got(gkr.at[pl.ds(0, nt - 1)], GK)
    mine = gkr[0].astype(F32)
    for i in range(1, nt):
        mine = mine + gkr[i].astype(F32)
    gkv[t] = mine.astype(BF)
    to_peers(lambda o: gkv.at[t], gkv, GKV)

    got(mix_f.at[pl.ds(0, nt - 1)], MIXF)
    added = mm(side_by_side(mix_f, 0, nt), wot[...].reshape(nt * HEAD, part))
    y[...] = (x[...].astype(F32) + added).astype(BF)

    @pl.when(s < n_pipe - 1)
    def _():
        send(y, next_out, NEXT, {"pipe": s + 1})

    @pl.when(s == 0)
    def _():
        pltpu.make_async_copy(zero, next_out, sem_r.at[NEXT]).start()

    got(gr.at[0], GRAD)
    got(mixb, MIXB)
    for_out = mm_at(side_by_side(mixb.at[0], 0, 4), gr[0]) + mm_at(
        side_by_side(mixb.at[1], 0, 4), gr[1]
    )
    columns = pl.ds(pl.multiple_of(seat * part, part), part)
    for i in range(4):
        wog[i] = for_out[i * HEAD : (i + 1) * HEAD].astype(BF)
        target = 4 * d + i
        self_too = jnp.logical_and(target == t, home == d)

        @pl.when(jnp.logical_not(self_too))
        def _():
            send(wog.at[i], gwo_out.at[:, columns], WOG, {"tensor": target, "dp": home})

        @pl.when(self_too)
        def _():
            pltpu.make_async_copy(wog.at[i], gwo_out.at[:, columns], sem_r.at[WOG]).start()

    got(gq.at[pl.ds(0, nt - 1)], GQ)
    send(gq.at[pl.ds(4 * sib, 4)], gq_sib, GQS, {"dp": sib})
    got(gkv.at[pl.ds(0, nt - 1)], GKV)
    send(gkv, gkv_sib, GKVS, {"dp": sib})
    gkv_all = gkv[...].reshape(rows, 2 * HEAD)
    gnorm = mm_bt(side_by_side(gq, 0, 4), wq[0]) + mm_bt(side_by_side(gq, 4, 4), wq[1])
    gnorm = gnorm + mm_bt(gkv_all, wkv[...])
    scaled = gnorm * wide
    gx[...] = (gr[d].astype(F32) + scaled * gain).astype(BF)

    @pl.when(s > 0)
    def _():
        send(gx, prev_out, PREV, {"pipe": s - 1})

    @pl.when(s == n_pipe - 1)
    def _():
        pltpu.make_async_copy(zero, prev_out, sem_r.at[PREV]).start()

    gn[...] = jnp.broadcast_to(jnp.sum(scaled * saved_f, axis=0, keepdims=True), gn.shape)
    send(gn, gn_sib, GN, {"dp": sib})

    got(nb_sib, NB)
    got(gkv_sib, GKVS)
    gwkv[...] = mm_at(nb[...], gkv_all) + mm_at(nb_sib[...], gkv_sib[...].reshape(rows, 2 * HEAD))
    out_kv = pltpu.make_async_copy(gwkv, gwkv_out, local_sem.at[5])
    out_kv.start()
    got(gq_sib, GQS)
    mine = jnp.concatenate([gq[4 * d + i] for i in range(4)], axis=1)
    gwq[...] = (mm_at(nb[...], mine) + mm_at(nb_sib[...], side_by_side(gq_sib, 0, 4))).astype(BF)
    out_q = pltpu.make_async_copy(gwq, gwq_out, local_sem.at[6])
    out_q.start()
    got(gn_sib, GN)
    gain_out[...] = gn[0:1] + gn_sib[0:1]

    sent(saved, MIRROR)
    sent(wq.at[0], WQ)
    for j in range(4):

        @pl.when(4 * d + j != t)
        def _():
            sent(wot.at[0], WOT)

    @pl.when(home == d)
    def _():
        sent(wot, FWD)

    sent(gr.at[0], GRAD)
    seven = pl.ds(0, nt - 1)
    for ref, index in (
        (qs_f, QF), (qs_b, QB), (ks_f, KF), (ks_b, KB), (sr_f, SF), (sr_b, SB), (kv_f, KVF),
        (kv_b, KVB), (gms, GM), (mix_f, MIXF), (gks, GK), (gkv, GKV), (gq, GQ), (gq, MIXB),
    ):
        sent(ref.at[seven], index)

    @pl.when(home != d)
    def _():
        sent(mixb_own, MIXB)

    sent(gq_sib, GQS)
    sent(gkv_sib, GKVS)
    sent(nb, NB)
    sent(gn, GN)

    @pl.when(s < n_pipe - 1)
    def _():
        sent(y, NEXT)

    @pl.when(s > 0)
    def _():
        sent(gx, PREV)

    for i in range(4):

        @pl.when(jnp.logical_not(jnp.logical_and(4 * d + i == t, home == d)))
        def _():
            sent(wog.at[i], WOG)

    got(gwo_out, WOG)
    got(next_out, NEXT)
    got(prev_out, PREV)
    out_kv.wait()
    out_q.wait()


def local(fwd_in, parked, grad_in, positions, kv_cache, w_query, w_keyval, w_out, gain):
    n_pipe = lax.axis_size("pipe")
    nt = lax.axis_size("tensor")
    rows, feat = fwd_in.shape[1:]
    span = kv_cache.shape[3]
    sub = rows // nt
    part = w_out.shape[2] // 4
    any_ = pl.BlockSpec(memory_space=pl.ANY)
    vmem = pl.BlockSpec(memory_space=pltpu.VMEM)

    def V(*shape, dtype=BF):
        return pltpu.VMEM(shape, dtype)

    heads = (nt, rows, HEAD)
    strips = (nt, sub, 2 * HEAD)
    sums = (nt, 8, rows)
    out = pl.pallas_call(
        functools.partial(kernel, n_pipe, feat * nt),
        out_shape=(
            jax.ShapeDtypeStruct((rows, feat), BF),
            jax.ShapeDtypeStruct((rows, feat), BF),
            jax.ShapeDtypeStruct(w_query.shape[1:], BF),
            jax.ShapeDtypeStruct(w_keyval.shape[1:], F32),
            jax.ShapeDtypeStruct(w_out.shape[1:], BF),
            jax.ShapeDtypeStruct((1, feat), F32),
        ),
        in_specs=[pl.BlockSpec(memory_space=pltpu.SMEM), vmem] + [any_] * 7,
        out_specs=(any_,) * 5 + (vmem,),
        scratch_shapes=[
            V(rows, feat), V(rows, feat), V(2, rows, feat), V(2, span, 2 * HEAD),
            V(2, *w_query.shape[1:]), V(*w_keyval.shape[1:]), V(nt, HEAD, part),
            V(*heads), V(*heads), V(*heads), V(*heads),
            V(*strips), V(*strips), V(*strips), V(*strips),
            V(8, rows, dtype=F32), V(*sums, dtype=F32), V(8, rows, dtype=F32), V(*sums, dtype=F32),
            V(*strips), V(*strips), V(rows, HEAD, dtype=F32), V(rows, HEAD, dtype=F32),
            V(*heads), V(*heads), V(*heads), V(rows, HEAD), V(2, 4, rows, HEAD),
            V(*strips), V(*strips), V(*strips), V(*heads), V(4, rows, HEAD), V(*strips),
            V(rows, feat), V(rows, feat),
            V(rows, feat), V(rows, feat), V(rows, feat), V(4, HEAD, part),
            V(*w_query.shape[1:]), V(*w_keyval.shape[1:], dtype=F32),
            V(8, feat, dtype=F32), V(8, feat, dtype=F32),
            pltpu.SemaphoreType.DMA((7,)),
            pltpu.SemaphoreType.DMA((8,)),
            pltpu.SemaphoreType.DMA((26,)),
            pltpu.SemaphoreType.DMA((26,)),
        ],
        compiler_params=pltpu.CompilerParams(
            collective_id=0, has_side_effects=True, vmem_limit_bytes=50 * 1024 * 1024
        ),
        name="relay",
    )(
        positions.reshape(2), gain, fwd_in[0], parked[0], grad_in[0], kv_cache[0, 0],
        w_query[0], w_keyval[0], w_out[0],
    )
    next_act, prev_grad, gwq, gwkv, gwo, ggain = out
    return next_act[None], prev_grad[None], gwq[None], gwkv[None], gwo[None], ggain


def solution(mesh):
    return jax.shard_map(
        local,
        mesh=mesh,
        in_specs=(
            P("pipe", "dp", "tensor"),
            P("pipe", "dp", "tensor"),
            P("pipe", "dp", "tensor"),
            P("pipe", "dp", None),
            P("pipe", "dp", None, None, None),
            P("pipe", "tensor", "dp"),
            P("pipe", "tensor", None),
            P("pipe", "tensor", "dp"),
            P("pipe", "tensor"),
        ),
        out_specs=(
            P("pipe", "dp", "tensor"),
            P("pipe", "dp", "tensor"),
            P("pipe", "tensor", "dp"),
            P("pipe", "tensor", None),
            P("pipe", "tensor", "dp"),
            P("pipe", "tensor"),
        ),
        check_vma=False,
    )
```

```python
import functools
import math

import jax
import jax.numpy as jnp
from jax import lax
from jax.experimental import pallas as pl
from jax.experimental.pallas import tpu as pltpu
from jax.sharding import PartitionSpec as P

HEAD = 128
MESH = pl.DeviceIdType.MESH
eps = 1e-05
BF = jnp.bfloat16
F32 = jnp.float32


def mm(a, b):
    return lax.dot_general(a, b, (((1,), (0,)), ((), ())), preferred_element_type=F32)


def mm_bt(a, b):
    return lax.dot_general(a, b, (((1,), (1,)), ((), ())), preferred_element_type=F32)


def mm_at(a, b):
    return lax.dot_general(a, b, (((0,), (0,)), ((), ())), preferred_element_type=F32)


def drain(ref, sem):
    pltpu.make_async_copy(ref, ref, sem).wait()


def side_by_side(ref, first, count):
    return jnp.concatenate([ref[first + i] for i in range(count)], axis=1)


def softmax_parts(q, kc, ko, live):
    rows, span = q.shape[0], kc.shape[0]
    factor = 1.0 / math.sqrt(HEAD)
    sc = mm_bt(q, kc) * factor
    so = mm_bt(q, ko) * factor
    col = lax.broadcasted_iota(jnp.int32, sc.shape, 1)
    sc = jnp.where(col >= span - live, sc, -1e30)
    col = lax.broadcasted_iota(jnp.int32, so.shape, 1)
    line = lax.broadcasted_iota(jnp.int32, so.shape, 0)
    so = jnp.where(col <= line, so, -1e30)
    top = jnp.maximum(jnp.max(sc, axis=1, keepdims=True), jnp.max(so, axis=1, keepdims=True))
    ec, eo = jnp.exp(sc - top), jnp.exp(so - top)
    total = jnp.sum(ec, axis=1, keepdims=True) + jnp.sum(eo, axis=1, keepdims=True)
    inverse = 1.0 / total
    return ec * inverse, eo * inverse


def kernel(
    n_pipe,
    width,
    pos_hbm, gain_hbm, x_hbm, parked_hbm, grad_hbm, cache_hbm, wq_hbm, wkv_hbm, wo_hbm,
    next_out, prev_out, gwq_out, gwkv_out, gwo_out, gain_out,
    x, saved, gr, cache, wq, wkv, wot,
    qs_f, qr_f, qs_b, qr_b, ks_f, kr_f, ks_b, kr_b, ss_f, sr_f, ss_b, sr_b,
    kv_f, kv_b, scale_f, scale_b, gms, gmr, mix_f, mixb_own, mixb,
    gks, gkr, gkv, gq, gq_sib, gkv_sib, nb, nb_sib,
    y, gx, zero, wog, gn, gn_sib,
    pos, gain_ref, local_sem, wot_sem, sem_s, sem_r,
):
    s, t, d = lax.axis_index("pipe"), lax.axis_index("tensor"), lax.axis_index("dp")
    sib = 1 - d
    home = t // 4
    nt = 8
    rows = x.shape[0]
    parts_b = qs_b.shape[0]

    barrier = pltpu.get_barrier_semaphore()
    mirror = n_pipe - 1 - s
    for stage in (mirror, lax.rem(s + 1, n_pipe), lax.rem(s + n_pipe - 1, n_pipe)):
        pl.semaphore_signal(barrier, inc=1, device_id={"pipe": stage}, device_id_type=MESH)
    for k in range(1, nt):
        other = lax.rem(t + k, nt)
        pl.semaphore_signal(barrier, inc=1, device_id={"tensor": other}, device_id_type=MESH)
        pl.semaphore_signal(
            barrier, inc=1, device_id={"tensor": other, "dp": sib}, device_id_type=MESH
        )
    pl.semaphore_signal(barrier, inc=1, device_id={"dp": sib}, device_id_type=MESH)

    loads = [
        pltpu.make_async_copy(x_hbm, x, local_sem.at[0]),
        pltpu.make_async_copy(wkv_hbm, wkv, local_sem.at[2]),
        pltpu.make_async_copy(wq_hbm, wq.at[d], local_sem.at[1]),
        pltpu.make_async_copy(grad_hbm, gr.at[d], local_sem.at[3]),
        pltpu.make_async_copy(cache_hbm, cache, local_sem.at[4]),
        pltpu.make_async_copy(gain_hbm, gain_ref, local_sem.at[5]),
        pltpu.make_async_copy(pos_hbm, pos, local_sem.at[6]),
    ]
    for load in loads:
        load.start()
    zero[...] = jnp.zeros_like(zero)

    pl.semaphore_wait(barrier, 2 * (nt - 1) + 1 + 3)

    names = (
        "WQ", "WOT", "FWD", "GRAD", "QF", "KF", "SF", "KVF", "GM", "MIXF", "MIXB", "GK", "GKV", "GQ",
        "GQS", "GKVS", "NB", "GN", "NEXT", "PREV", "WOG",
    )
    at = {name: i for i, name in enumerate(names)}
    index_of = len(names)
    for name in ("MIRROR", "QB", "KB", "SB", "KVB"):
        for c in range(parts_b):
            at[name, c] = index_of
            index_of += 1

    def send(src, dst, name, device, rsem=None):
        pltpu.make_async_remote_copy(
            src_ref=src,
            dst_ref=dst,
            send_sem=sem_s.at[at[name]],
            recv_sem=sem_r.at[at[name]] if rsem is None else rsem,
            device_id=device,
            device_id_type=MESH,
        ).start()

    def got(ref, name):
        drain(ref, sem_r.at[at[name]])

    def sent(ref, name):
        drain(ref, sem_s.at[at[name]])

    def to_peers(src_of, dst, name):
        for k in range(1, nt):
            other = lax.rem(t + k, nt)
            send(src_of(other), dst.at[t], name, {"tensor": other})

    seven = pl.ds(0, nt - 1)

    chunk = rows // parts_b
    for c in range(parts_b):
        cut = pl.ds(c * chunk, chunk)
        send(parked_hbm.at[cut], saved.at[cut], ("MIRROR", c), {"pipe": mirror})
    send(wq_hbm, wq.at[d], "WQ", {"dp": sib})
    part = wo_hbm.shape[1] // 4
    for j in range(4):
        target = 4 * d + j
        block = wo_hbm.at[:, pl.ds(j * part, part)]

        @pl.when(target != t)
        def _():
            send(block, wot.at[t], "WOT", {"tensor": target}, wot_sem.at[t])

        @pl.when(target == t)
        def _():
            pltpu.make_async_copy(block, wot.at[t], wot_sem.at[t]).start()

    def project(data, qs, qr, ks, kr, ss, sr, names, ready=None):
        sub = ks.shape[1]
        xf = data.astype(F32)
        xg = (xf * gain).astype(BF)
        value = mm(xg, wkv[...]).astype(BF)
        for i in range(nt):
            ks[i] = value[i * sub : (i + 1) * sub]
        to_peers(lambda o: ks.at[o], kr, names[1])
        sq = xf * xf
        quarter = sq[:, :HEAD]
        for i in range(1, sq.shape[1] // HEAD):
            quarter = quarter + sq[:, i * HEAD : (i + 1) * HEAD]
        row = jnp.sum(quarter.T, axis=0, keepdims=True)
        ss[...] = jnp.broadcast_to(row, ss.shape)
        to_peers(lambda o: ss, sr, names[2])
        if ready is not None:
            ready()
        for half in range(2):
            value = mm(xg, wq[half])
            for i in range(4):
                qs[4 * half + i] = value[:, i * HEAD : (i + 1) * HEAD].astype(BF)
        to_peers(lambda o: qs.at[o], qr, names[0])
        qr[t] = qs[t]
        kr[t] = ks[t]
        sr[t] = ss[...]

    def combine_keyval(kr, sr, kv, scale, names):
        sub = kr.shape[1]
        got(sr.at[seven], names[2])
        totals = sr[0]
        for i in range(1, nt):
            totals = totals + sr[i]
        row = lax.rsqrt(totals / width + eps)[0:1]
        scale[...] = jnp.broadcast_to(row, (HEAD, row.shape[1])).T
        got(kr.at[seven], names[1])
        mine = kr[0].astype(F32)
        for i in range(1, nt):
            mine = mine + kr[i].astype(F32)
        part_scale = scale[pl.ds(pl.multiple_of(t * sub, sub), sub), :]
        kv[t] = (mine * jnp.concatenate([part_scale, part_scale], axis=1)).astype(BF)
        to_peers(lambda o: kv.at[t], kv, names[3])

    def combine_query(qr, scale, names):
        got(qr.at[seven], names[0])
        q = qr[0].astype(F32)
        for i in range(1, nt):
            q = q + qr[i].astype(F32)
        return (q * scale[...]).astype(BF)

    names_f = ("QF", "KF", "SF", "KVF")

    def ready():
        loads[2].wait()
        got(wq.at[0], "WQ")

    loads[0].wait()
    loads[1].wait()
    loads[5].wait()
    gain = gain_ref[...].astype(F32)
    project(x[...], qs_f, qr_f, ks_f, kr_f, ss_f, sr_f, names_f, ready)

    send(grad_hbm, gr.at[d], "GRAD", {"dp": sib})
    names_b = [(("QB", c), ("KB", c), ("SB", c), ("KVB", c)) for c in range(parts_b)]
    for c in range(parts_b):
        cut = pl.ds(c * chunk, chunk)
        got(saved.at[cut], ("MIRROR", c))
        project(
            saved[cut], qs_b.at[c], qr_b.at[c], ks_b.at[c], kr_b.at[c], ss_b.at[c], sr_b.at[c],
            names_b[c],
        )
        if c == 0:
            loads[3].wait()
            for h in range(nt):
                drain(wot.at[h], wot_sem.at[h])

                @pl.when(home == d)
                def _():
                    send(wot.at[h], wot.at[h], "FWD", {"dp": sib}, wot_sem.at[h])

    combine_keyval(kr_f, sr_f, kv_f, scale_f, names_f)
    grad = gr[d]
    for h in range(nt):
        gms[h] = mm_bt(grad, wot[h]).astype(BF)
    to_peers(lambda o: gms.at[o], gmr, "GM")
    gmr[t] = gms[t]

    q_f = combine_query(qr_f, scale_f, names_f)
    for c in range(parts_b):
        combine_keyval(kr_b.at[c], sr_b.at[c], kv_b.at[c], scale_b.at[c], names_b[c])

    loads[4].wait()
    loads[6].wait()
    got(kv_f.at[seven], "KVF")
    span = cache.shape[1]
    own = kv_f[...].reshape(rows, 2 * HEAD)
    live = jnp.minimum(pos[0, 0], span)
    wc, wo_ = softmax_parts(q_f, cache[0, :, :HEAD], own[:, :HEAD], live)
    mixed = mm(wc.astype(BF), cache[0, :, HEAD:]) + mm(wo_.astype(BF), own[:, HEAD:])
    mix_f[t] = mixed.astype(BF)
    to_peers(lambda o: mix_f.at[t], mix_f, "MIXF")

    q_b = jnp.concatenate(
        [combine_query(qr_b.at[c], scale_b.at[c], names_b[c]) for c in range(parts_b)], axis=0
    )
    for c in range(parts_b):
        got(kv_b.at[c, seven], ("KVB", c))
    own = kv_b[...].reshape(rows, 2 * HEAD)
    live = jnp.minimum(pos[0, 1], span)
    kc, vc, ko, vo = cache[1, :, :HEAD], cache[1, :, HEAD:], own[:, :HEAD], own[:, HEAD:]
    wc, wo_ = softmax_parts(q_b, kc, ko, live)
    pc, po = wc.astype(BF), wo_.astype(BF)

    mixb_own[...] = (mm(pc, vc) + mm(po, vo)).astype(BF)
    seat = lax.rem(t, 4)
    for k in range(nt):
        other = lax.rem(t + k, nt)
        if k == 0:

            @pl.when(home != d)
            def _():
                send(mixb_own, mixb.at[d, seat], "MIXB", {"dp": sib})

            @pl.when(home == d)
            def _():
                pltpu.make_async_copy(mixb_own, mixb.at[d, seat], sem_r.at[at["MIXB"]]).start()

        else:
            send(mixb_own, mixb.at[d, seat], "MIXB", {"tensor": other, "dp": home})


    got(gmr.at[seven], "GM")
    gm = gmr[0].astype(F32)
    for i in range(1, nt):
        gm = gm + gmr[i].astype(F32)
    gm = gm.astype(BF)
    gpc, gpo = mm_bt(gm, vc), mm_bt(gm, vo)
    mean = jnp.sum(gpc * wc, axis=1, keepdims=True) + jnp.sum(gpo * wo_, axis=1, keepdims=True)
    factor = 1.0 / math.sqrt(HEAD)
    gso = (wo_ * (gpo - mean) * factor).astype(BF)
    gkeys = mm_at(gso, q_b).astype(BF)
    gvals = mm_at(po, gm).astype(BF)
    sub = rows // nt
    for i in range(nt):
        gks[i, :, :HEAD] = gkeys[i * sub : (i + 1) * sub]
        gks[i, :, HEAD:] = gvals[i * sub : (i + 1) * sub]
    to_peers(lambda o: gks.at[o], gkr, "GK")
    gkr[t] = gks[t]
    gsc = (wc * (gpc - mean) * factor).astype(BF)
    gq[t] = (mm(gsc, kc) + mm(gso, ko)).astype(BF)
    to_peers(lambda o: gq.at[t], gq, "GQ")

    saved_f = saved[...].astype(F32)
    scale = scale_b[...].reshape(rows, HEAD)
    wide = jnp.concatenate([scale] * (saved.shape[1] // HEAD), axis=1)
    nb[...] = (saved_f * wide * gain).astype(BF)
    send(nb, nb_sib, "NB", {"dp": sib})

    got(mix_f.at[seven], "MIXF")
    added = mm(side_by_side(mix_f, 0, nt), wot[...].reshape(nt * HEAD, part))
    y[...] = (x[...].astype(F32) + added).astype(BF)

    @pl.when(s < n_pipe - 1)
    def _():
        send(y, next_out, "NEXT", {"pipe": s + 1})

    @pl.when(s == 0)
    def _():
        pltpu.make_async_copy(zero, next_out, sem_r.at[at["NEXT"]]).start()

    got(gkr.at[seven], "GK")
    mine = gkr[0].astype(F32)
    for i in range(1, nt):
        mine = mine + gkr[i].astype(F32)
    gkv[t] = mine.astype(BF)
    to_peers(lambda o: gkv.at[t], gkv, "GKV")

    got(gr.at[0], "GRAD")
    got(mixb, "MIXB")
    for_out = mm_at(side_by_side(mixb.at[0], 0, 4), gr[0]) + mm_at(
        side_by_side(mixb.at[1], 0, 4), gr[1]
    )
    columns = pl.ds(pl.multiple_of(seat * part, part), part)
    for i in range(4):
        wog[i] = for_out[i * HEAD : (i + 1) * HEAD].astype(BF)
        target = 4 * d + i
        self_too = jnp.logical_and(target == t, home == d)

        @pl.when(jnp.logical_not(self_too))
        def _():
            send(wog.at[i], gwo_out.at[:, columns], "WOG", {"tensor": target, "dp": home})

        @pl.when(self_too)
        def _():
            pltpu.make_async_copy(
                wog.at[i], gwo_out.at[:, columns], sem_r.at[at["WOG"]]
            ).start()

    got(gq.at[seven], "GQ")
    send(gq.at[pl.ds(4 * sib, 4)], gq_sib, "GQS", {"dp": sib})
    gnorm = mm_bt(side_by_side(gq, 0, 4), wq[0]) + mm_bt(side_by_side(gq, 4, 4), wq[1])
    got(gkv.at[seven], "GKV")
    send(gkv, gkv_sib, "GKVS", {"dp": sib})
    gkv_all = gkv[...].reshape(rows, 2 * HEAD)
    scaled = (gnorm + mm_bt(gkv_all, wkv[...])) * wide
    gx[...] = (gr[d].astype(F32) + scaled * gain).astype(BF)

    @pl.when(s > 0)
    def _():
        send(gx, prev_out, "PREV", {"pipe": s - 1})

    @pl.when(s == n_pipe - 1)
    def _():
        pltpu.make_async_copy(zero, prev_out, sem_r.at[at["PREV"]]).start()

    gn[...] = jnp.broadcast_to(jnp.sum(scaled * saved_f, axis=0, keepdims=True), gn.shape)
    send(gn, gn_sib, "GN", {"dp": sib})

    got(nb_sib, "NB")
    got(gkv_sib, "GKVS")
    gwkv_out[...] = mm_at(nb[...], gkv_all) + mm_at(
        nb_sib[...], gkv_sib[...].reshape(rows, 2 * HEAD)
    )
    got(gq_sib, "GQS")
    mine = jnp.concatenate([gq[4 * d + i] for i in range(4)], axis=1)
    gwq_out[...] = (
        mm_at(nb[...], mine) + mm_at(nb_sib[...], side_by_side(gq_sib, 0, 4))
    ).astype(BF)
    got(gn_sib, "GN")
    gain_out[...] = gn[0:1] + gn_sib[0:1]

    for c in range(parts_b):
        cut = pl.ds(c * chunk, chunk)
        sent(saved.at[cut], ("MIRROR", c))
        sent(qs_b.at[c, seven], ("QB", c))
        sent(ks_b.at[c, seven], ("KB", c))
        sent(sr_b.at[c, seven], ("SB", c))
        sent(kv_b.at[c, seven], ("KVB", c))
    sent(wq.at[0], "WQ")
    for j in range(4):

        @pl.when(4 * d + j != t)
        def _():
            sent(wot.at[0], "WOT")

    @pl.when(home == d)
    def _():
        sent(wot, "FWD")

    sent(gr.at[0], "GRAD")
    for ref, name in (
        (qs_f, "QF"), (ks_f, "KF"), (sr_f, "SF"), (kv_f, "KVF"), (gms, "GM"), (mix_f, "MIXF"),
        (gks, "GK"), (gkv, "GKV"), (gq, "GQ"), (gq, "MIXB"),
    ):
        sent(ref.at[seven], name)

    @pl.when(home != d)
    def _():
        sent(mixb_own, "MIXB")

    sent(gq_sib, "GQS")
    sent(gkv_sib, "GKVS")
    sent(nb, "NB")
    sent(gn, "GN")

    @pl.when(s < n_pipe - 1)
    def _():
        sent(y, "NEXT")

    @pl.when(s > 0)
    def _():
        sent(gx, "PREV")

    for i in range(4):

        @pl.when(jnp.logical_not(jnp.logical_and(4 * d + i == t, home == d)))
        def _():
            sent(wog.at[i], "WOG")

    got(gwo_out, "WOG")
    got(next_out, "NEXT")
    got(prev_out, "PREV")


def place(*refs):
    count = len(refs) // 2
    sem = refs[-1]
    copies = [
        pltpu.make_async_copy(refs[i], refs[count + i], sem.at[i]) for i in range(count)
    ]
    for copy in copies:
        copy.start()
    for copy in copies:
        copy.wait()


def local(fwd_in, parked, grad_in, positions, kv_cache, w_query, w_keyval, w_out, gain):
    n_pipe = lax.axis_size("pipe")
    nt = lax.axis_size("tensor")
    rows, feat = fwd_in.shape[1:]
    span = kv_cache.shape[3]
    part = w_out.shape[2] // 4
    any_ = pl.BlockSpec(memory_space=pltpu.HBM)
    vmem = pl.BlockSpec(memory_space=pltpu.VMEM)

    def V(*shape, dtype=BF):
        return pltpu.VMEM(shape, dtype)

    parts_b = 2
    cut = rows // parts_b
    heads = (nt, rows, HEAD)
    heads_b = (parts_b, nt, cut, HEAD)
    strips = (nt, rows // nt, 2 * HEAD)
    strips_b = (parts_b, nt, cut // nt, 2 * HEAD)

    out = pl.pallas_call(
        functools.partial(kernel, n_pipe, feat * nt),
        out_shape=(
            pltpu.VMEM((rows, feat), BF),
            pltpu.VMEM((rows, feat), BF),
            pltpu.VMEM(w_query.shape[1:], BF),
            pltpu.VMEM(w_keyval.shape[1:], F32),
            pltpu.VMEM(w_out.shape[1:], BF),
            pltpu.VMEM((1, feat), F32),
        ),
        in_specs=[any_] * 9,
        out_specs=(vmem,) * 6,
        scratch_shapes=[
            V(rows, feat), V(rows, feat), V(2, rows, feat), V(2, span, 2 * HEAD),
            V(2, *w_query.shape[1:]), V(*w_keyval.shape[1:]), V(nt, HEAD, part),
            V(*heads), V(*heads), V(*heads_b), V(*heads_b),
            V(*strips), V(*strips), V(*strips_b), V(*strips_b),
            V(8, rows, dtype=F32), V(nt, 8, rows, dtype=F32),
            V(parts_b, 8, cut, dtype=F32), V(parts_b, nt, 8, cut, dtype=F32),
            V(*strips), V(*strips_b), V(rows, HEAD, dtype=F32), V(parts_b, cut, HEAD, dtype=F32),
            V(*heads), V(*heads), V(*heads), V(rows, HEAD), V(2, 4, rows, HEAD),
            V(*strips), V(*strips), V(*strips), V(*heads), V(4, rows, HEAD), V(*strips),
            V(rows, feat), V(rows, feat),
            V(rows, feat), V(rows, feat), V(rows, feat), V(4, HEAD, part),
            V(8, feat, dtype=F32), V(8, feat, dtype=F32),
            pltpu.SMEM((1, 2), jnp.int32), V(1, feat),
            pltpu.SemaphoreType.DMA((7,)),
            pltpu.SemaphoreType.DMA((8,)),
            pltpu.SemaphoreType.DMA((22 + 5 * parts_b,)),
            pltpu.SemaphoreType.DMA((22 + 5 * parts_b,)),
        ],
        compiler_params=pltpu.CompilerParams(
            collective_id=0, has_side_effects=True, vmem_limit_bytes=32 * 1024 * 1024
        ),
        name="relay",
    )(
        *(
            pltpu.with_memory_space_constraint(v, pltpu.HBM)
            for v in (
                positions[0], gain, fwd_in[0], parked[0], grad_in[0], kv_cache[0, 0], w_query[0], w_keyval[0], w_out[0]
            )
        ),
    )
    next_act, prev_grad, gwq, gwkv, gwo, ggain = pl.pallas_call(
        place,
        out_shape=tuple(jax.ShapeDtypeStruct(v.shape, v.dtype) for v in out),
        in_specs=[vmem] * len(out),
        out_specs=(any_,) * len(out),
        scratch_shapes=[pltpu.SemaphoreType.DMA((len(out),))],
        compiler_params=pltpu.CompilerParams(vmem_limit_bytes=4 * 1024 * 1024),
        name="place",
    )(*out)
    return next_act[None], prev_grad[None], gwq[None], gwkv[None], gwo[None], ggain


def solution(mesh):
    return jax.shard_map(
        local,
        mesh=mesh,
        in_specs=(
            P("pipe", "dp", "tensor"),
            P("pipe", "dp", "tensor"),
            P("pipe", "dp", "tensor"),
            P("pipe", "dp", None),
            P("pipe", "dp", None, None, None),
            P("pipe", "tensor", "dp"),
            P("pipe", "tensor", None),
            P("pipe", "tensor", "dp"),
            P("pipe", "tensor"),
        ),
        out_specs=(
            P("pipe", "dp", "tensor"),
            P("pipe", "dp", "tensor"),
            P("pipe", "tensor", "dp"),
            P("pipe", "tensor", None),
            P("pipe", "tensor", "dp"),
            P("pipe", "tensor"),
        ),
        check_vma=False,
    )
```

```python
import functools
import math

import jax
import jax.numpy as jnp
from jax import lax
from jax.experimental import pallas as pl
from jax.experimental.pallas import tpu as pltpu
from jax.sharding import PartitionSpec as P

HEAD = 128
MESH = pl.DeviceIdType.MESH
eps = 1e-05
BF = jnp.bfloat16
F32 = jnp.float32


def mm(a, b):
    return lax.dot_general(a, b, (((1,), (0,)), ((), ())), preferred_element_type=F32)


def mm_bt(a, b):
    return lax.dot_general(a, b, (((1,), (1,)), ((), ())), preferred_element_type=F32)


def mm_at(a, b):
    return lax.dot_general(a, b, (((0,), (0,)), ((), ())), preferred_element_type=F32)


def drain(ref, sem):
    pltpu.make_async_copy(ref, ref, sem).wait()


def side_by_side(ref, first, count):
    return jnp.concatenate([ref[first + i] for i in range(count)], axis=1)


def softmax_parts(q, kc, ko, live):
    rows, span = q.shape[0], kc.shape[0]
    factor = 1.0 / math.sqrt(HEAD)
    sc = mm_bt(q, kc) * factor
    so = mm_bt(q, ko) * factor
    col = lax.broadcasted_iota(jnp.int32, sc.shape, 1)
    sc = jnp.where(col >= span - live, sc, -1e30)
    col = lax.broadcasted_iota(jnp.int32, so.shape, 1)
    line = lax.broadcasted_iota(jnp.int32, so.shape, 0)
    so = jnp.where(col <= line, so, -1e30)
    top = jnp.maximum(jnp.max(sc, axis=1, keepdims=True), jnp.max(so, axis=1, keepdims=True))
    ec, eo = jnp.exp(sc - top), jnp.exp(so - top)
    total = jnp.sum(ec, axis=1, keepdims=True) + jnp.sum(eo, axis=1, keepdims=True)
    inverse = 1.0 / total
    return ec * inverse, eo * inverse


def kernel(
    n_pipe,
    width,
    pos_hbm, gain_hbm, x_hbm, parked_hbm, grad_hbm, cache_hbm, wq_hbm, wkv_hbm, wo_hbm,
    next_out, prev_out, gwq_out, gwkv_out, gwo_out, gain_out,
    x, saved, gr, cache, wq, wkv, wot,
    qs_f, qr_f, qs_b, qr_b, ks_f, kr_f, ks_b, kr_b, ss_f, sr_f, ss_b, sr_b,
    kv_f, kv_b, scale_f, scale_b, gms, gmr, mix_f, mixb_own, mixb,
    gks, gkr, gkv, gq, gq_sib, gkv_sib, nb, nb_sib,
    y, gx, zero, wog, gn, gn_sib,
    pos, gain_ref, local_sem, wot_sem, sem_s, sem_r,
):
    s, t, d = lax.axis_index("pipe"), lax.axis_index("tensor"), lax.axis_index("dp")
    sib = 1 - d
    home = t // 4
    nt = 8
    rows = x.shape[0]
    parts_b = qs_b.shape[0]

    barrier = pltpu.get_barrier_semaphore()
    mirror = n_pipe - 1 - s
    for stage in (mirror, lax.rem(s + 1, n_pipe), lax.rem(s + n_pipe - 1, n_pipe)):
        pl.semaphore_signal(barrier, inc=1, device_id={"pipe": stage}, device_id_type=MESH)
    for k in range(1, nt):
        other = lax.rem(t + k, nt)
        pl.semaphore_signal(barrier, inc=1, device_id={"tensor": other}, device_id_type=MESH)
        pl.semaphore_signal(
            barrier, inc=1, device_id={"tensor": other, "dp": sib}, device_id_type=MESH
        )
    pl.semaphore_signal(barrier, inc=1, device_id={"dp": sib}, device_id_type=MESH)

    loads = [
        pltpu.make_async_copy(x_hbm, x, local_sem.at[0]),
        pltpu.make_async_copy(wkv_hbm, wkv, local_sem.at[2]),
        pltpu.make_async_copy(wq_hbm, wq.at[d], local_sem.at[1]),
        pltpu.make_async_copy(grad_hbm, gr.at[d], local_sem.at[3]),
        pltpu.make_async_copy(cache_hbm, cache, local_sem.at[4]),
        pltpu.make_async_copy(gain_hbm, gain_ref, local_sem.at[5]),
        pltpu.make_async_copy(pos_hbm, pos, local_sem.at[6]),
    ]
    for load in loads:
        load.start()
    zero[...] = jnp.zeros_like(zero)

    pl.semaphore_wait(barrier, 2 * (nt - 1) + 1 + 3)

    names = (
        "WQ", "WOT", "FWD", "GRAD", "QF", "KF", "SF", "KVF", "GM", "MIXF", "MIXB", "GK", "GKV", "GQ",
        "GQS", "GKVS", "NB", "GN", "NEXT", "PREV", "WOG",
    )
    at = {name: i for i, name in enumerate(names)}
    index_of = len(names)
    for name in ("MIRROR", "QB", "KB", "SB", "KVB"):
        for c in range(parts_b):
            at[name, c] = index_of
            index_of += 1

    def send(src, dst, name, device, rsem=None):
        pltpu.make_async_remote_copy(
            src_ref=src,
            dst_ref=dst,
            send_sem=sem_s.at[at[name]],
            recv_sem=sem_r.at[at[name]] if rsem is None else rsem,
            device_id=device,
            device_id_type=MESH,
        ).start()

    def got(ref, name):
        drain(ref, sem_r.at[at[name]])

    def sent(ref, name):
        drain(ref, sem_s.at[at[name]])

    def to_peers(src_of, dst, name):
        for k in range(1, nt):
            other = lax.rem(t + k, nt)
            send(src_of(other), dst.at[t], name, {"tensor": other})

    seven = pl.ds(0, nt - 1)

    chunk = rows // parts_b
    for c in range(parts_b):
        cut = pl.ds(c * chunk, chunk)
        send(parked_hbm.at[cut], saved.at[cut], ("MIRROR", c), {"pipe": mirror})
    send(wq_hbm, wq.at[d], "WQ", {"dp": sib})
    part = wo_hbm.shape[1] // 4
    for j in range(4):
        target = 4 * d + j
        block = wo_hbm.at[:, pl.ds(j * part, part)]

        @pl.when(target != t)
        def _():
            send(block, wot.at[t], "WOT", {"tensor": target}, wot_sem.at[t])

        @pl.when(target == t)
        def _():
            pltpu.make_async_copy(block, wot.at[t], wot_sem.at[t]).start()

    def project(data, qs, qr, ks, kr, ss, sr, names, ready=None):
        sub = ks.shape[1]
        xf = data.astype(F32)
        xg = (xf * gain).astype(BF)
        value = mm(xg, wkv[...]).astype(BF)
        for i in range(nt):
            ks[i] = value[i * sub : (i + 1) * sub]
        to_peers(lambda o: ks.at[o], kr, names[1])
        sq = xf * xf
        quarter = sq[:, :HEAD]
        for i in range(1, sq.shape[1] // HEAD):
            quarter = quarter + sq[:, i * HEAD : (i + 1) * HEAD]
        row = jnp.sum(quarter.T, axis=0, keepdims=True)
        ss[...] = jnp.broadcast_to(row, ss.shape)
        to_peers(lambda o: ss, sr, names[2])
        if ready is not None:
            ready()
        for half in range(2):
            value = mm(xg, wq[half])
            for i in range(4):
                qs[4 * half + i] = value[:, i * HEAD : (i + 1) * HEAD].astype(BF)
            for i in range(4):
                head = 4 * half + lax.rem(t + i, 4)

                @pl.when(head != t)
                def _():
                    send(qs.at[head], qr.at[t], names[0], {"tensor": head})

        qr[t] = qs[t]
        kr[t] = ks[t]
        sr[t] = ss[...]

    def combine_keyval(kr, sr, kv, scale, names):
        sub = kr.shape[1]
        got(sr.at[seven], names[2])
        totals = sr[0]
        for i in range(1, nt):
            totals = totals + sr[i]
        row = lax.rsqrt(totals / width + eps)[0:1]
        scale[...] = jnp.broadcast_to(row, (HEAD, row.shape[1])).T
        got(kr.at[seven], names[1])
        mine = kr[0].astype(F32)
        for i in range(1, nt):
            mine = mine + kr[i].astype(F32)
        part_scale = scale[pl.ds(pl.multiple_of(t * sub, sub), sub), :]
        kv[t] = (mine * jnp.concatenate([part_scale, part_scale], axis=1)).astype(BF)
        to_peers(lambda o: kv.at[t], kv, names[3])

    def combine_query(qr, scale, names):
        got(qr.at[seven], names[0])
        q = qr[0].astype(F32)
        for i in range(1, nt):
            q = q + qr[i].astype(F32)
        return (q * scale[...]).astype(BF)

    names_f = ("QF", "KF", "SF", "KVF")

    def ready():
        loads[2].wait()
        got(wq.at[0], "WQ")

    loads[0].wait()
    loads[1].wait()
    loads[5].wait()
    gain = gain_ref[...].astype(F32)
    project(x[...], qs_f, qr_f, ks_f, kr_f, ss_f, sr_f, names_f, ready)

    send(grad_hbm, gr.at[d], "GRAD", {"dp": sib})
    names_b = [(("QB", c), ("KB", c), ("SB", c), ("KVB", c)) for c in range(parts_b)]
    for c in range(parts_b):
        cut = pl.ds(c * chunk, chunk)
        got(saved.at[cut], ("MIRROR", c))
        project(
            saved[cut], qs_b.at[c], qr_b.at[c], ks_b.at[c], kr_b.at[c], ss_b.at[c], sr_b.at[c],
            names_b[c],
        )
        if c == 0:
            loads[3].wait()
            for h in range(nt):
                drain(wot.at[h], wot_sem.at[h])

                @pl.when(home == d)
                def _():
                    send(wot.at[h], wot.at[h], "FWD", {"dp": sib}, wot_sem.at[h])

    combine_keyval(kr_f, sr_f, kv_f, scale_f, names_f)
    combine_keyval(kr_b.at[0], sr_b.at[0], kv_b.at[0], scale_b.at[0], names_b[0])
    grad = gr[d]
    for k in range(1, nt):
        other = lax.rem(t + k, nt)
        gms[other] = mm_bt(grad, wot[other]).astype(BF)
        send(gms.at[other], gmr.at[t], "GM", {"tensor": other})
    gmr[t] = mm_bt(grad, wot[t]).astype(BF)

    q_f = combine_query(qr_f, scale_f, names_f)
    for c in range(1, parts_b):
        combine_keyval(kr_b.at[c], sr_b.at[c], kv_b.at[c], scale_b.at[c], names_b[c])

    loads[4].wait()
    loads[6].wait()
    got(kv_f.at[seven], "KVF")
    span = cache.shape[1]
    own = kv_f[...].reshape(rows, 2 * HEAD)
    live = jnp.minimum(pos[0, 0], span)
    wc, wo_ = softmax_parts(q_f, cache[0, :, :HEAD], own[:, :HEAD], live)
    mixed = mm(wc.astype(BF), cache[0, :, HEAD:]) + mm(wo_.astype(BF), own[:, HEAD:])
    mix_f[t] = mixed.astype(BF)
    to_peers(lambda o: mix_f.at[t], mix_f, "MIXF")

    q_b = jnp.concatenate(
        [combine_query(qr_b.at[c], scale_b.at[c], names_b[c]) for c in range(parts_b)], axis=0
    )
    for c in range(parts_b):
        got(kv_b.at[c, seven], ("KVB", c))
    own = kv_b[...].reshape(rows, 2 * HEAD)
    live = jnp.minimum(pos[0, 1], span)
    kc, vc, ko, vo = cache[1, :, :HEAD], cache[1, :, HEAD:], own[:, :HEAD], own[:, HEAD:]
    wc, wo_ = softmax_parts(q_b, kc, ko, live)
    pc, po = wc.astype(BF), wo_.astype(BF)

    mixb_own[...] = (mm(pc, vc) + mm(po, vo)).astype(BF)
    seat = lax.rem(t, 4)
    for k in range(nt):
        other = lax.rem(t + k, nt)
        if k == 0:

            @pl.when(home != d)
            def _():
                send(mixb_own, mixb.at[d, seat], "MIXB", {"dp": sib})

            @pl.when(home == d)
            def _():
                pltpu.make_async_copy(mixb_own, mixb.at[d, seat], sem_r.at[at["MIXB"]]).start()

        else:
            send(mixb_own, mixb.at[d, seat], "MIXB", {"tensor": other, "dp": home})


    got(gmr.at[seven], "GM")
    gm = gmr[0].astype(F32)
    for i in range(1, nt):
        gm = gm + gmr[i].astype(F32)
    gm = gm.astype(BF)
    gpc, gpo = mm_bt(gm, vc), mm_bt(gm, vo)
    mean = jnp.sum(gpc * wc, axis=1, keepdims=True) + jnp.sum(gpo * wo_, axis=1, keepdims=True)
    factor = 1.0 / math.sqrt(HEAD)
    gso = (wo_ * (gpo - mean) * factor).astype(BF)
    gkeys = mm_at(gso, q_b).astype(BF)
    gvals = mm_at(po, gm).astype(BF)
    sub = rows // nt
    for i in range(nt):
        gks[i, :, :HEAD] = gkeys[i * sub : (i + 1) * sub]
        gks[i, :, HEAD:] = gvals[i * sub : (i + 1) * sub]
    to_peers(lambda o: gks.at[o], gkr, "GK")
    gkr[t] = gks[t]
    gsc = (wc * (gpc - mean) * factor).astype(BF)
    gq[t] = (mm(gsc, kc) + mm(gso, ko)).astype(BF)
    to_peers(lambda o: gq.at[t], gq, "GQ")

    saved_f = saved[...].astype(F32)
    scale = scale_b[...].reshape(rows, HEAD)
    wide = jnp.concatenate([scale] * (saved.shape[1] // HEAD), axis=1)
    nb[...] = (saved_f * wide * gain).astype(BF)
    send(nb, nb_sib, "NB", {"dp": sib})

    got(mix_f.at[seven], "MIXF")
    added = mm(side_by_side(mix_f, 0, nt), wot[...].reshape(nt * HEAD, part))
    y[...] = (x[...].astype(F32) + added).astype(BF)

    @pl.when(s < n_pipe - 1)
    def _():
        send(y, next_out, "NEXT", {"pipe": s + 1})

    @pl.when(s == 0)
    def _():
        pltpu.make_async_copy(zero, next_out, sem_r.at[at["NEXT"]]).start()

    got(gkr.at[seven], "GK")
    mine = gkr[0].astype(F32)
    for i in range(1, nt):
        mine = mine + gkr[i].astype(F32)
    gkv[t] = mine.astype(BF)
    to_peers(lambda o: gkv.at[t], gkv, "GKV")

    got(gr.at[0], "GRAD")
    got(mixb, "MIXB")
    for_out = mm_at(side_by_side(mixb.at[0], 0, 4), gr[0]) + mm_at(
        side_by_side(mixb.at[1], 0, 4), gr[1]
    )
    columns = pl.ds(pl.multiple_of(seat * part, part), part)
    for i in range(4):
        wog[i] = for_out[i * HEAD : (i + 1) * HEAD].astype(BF)
        target = 4 * d + i
        self_too = jnp.logical_and(target == t, home == d)

        @pl.when(jnp.logical_not(self_too))
        def _():
            send(wog.at[i], gwo_out.at[:, columns], "WOG", {"tensor": target, "dp": home})

        @pl.when(self_too)
        def _():
            pltpu.make_async_copy(
                wog.at[i], gwo_out.at[:, columns], sem_r.at[at["WOG"]]
            ).start()

    got(gq.at[seven], "GQ")
    send(gq.at[pl.ds(4 * sib, 4)], gq_sib, "GQS", {"dp": sib})
    gnorm = mm_bt(side_by_side(gq, 0, 4), wq[0]) + mm_bt(side_by_side(gq, 4, 4), wq[1])
    got(gkv.at[seven], "GKV")
    send(gkv, gkv_sib, "GKVS", {"dp": sib})
    gkv_all = gkv[...].reshape(rows, 2 * HEAD)
    scaled = (gnorm + mm_bt(gkv_all, wkv[...])) * wide
    gx[...] = (gr[d].astype(F32) + scaled * gain).astype(BF)

    @pl.when(s > 0)
    def _():
        send(gx, prev_out, "PREV", {"pipe": s - 1})

    @pl.when(s == n_pipe - 1)
    def _():
        pltpu.make_async_copy(zero, prev_out, sem_r.at[at["PREV"]]).start()

    gn[...] = jnp.broadcast_to(jnp.sum(scaled * saved_f, axis=0, keepdims=True), gn.shape)
    send(gn, gn_sib, "GN", {"dp": sib})

    got(nb_sib, "NB")
    got(gkv_sib, "GKVS")
    gwkv_out[...] = mm_at(nb[...], gkv_all) + mm_at(
        nb_sib[...], gkv_sib[...].reshape(rows, 2 * HEAD)
    )
    got(gq_sib, "GQS")
    mine = jnp.concatenate([gq[4 * d + i] for i in range(4)], axis=1)
    gwq_out[...] = (
        mm_at(nb[...], mine) + mm_at(nb_sib[...], side_by_side(gq_sib, 0, 4))
    ).astype(BF)
    got(gn_sib, "GN")
    gain_out[...] = gn[0:1] + gn_sib[0:1]

    for c in range(parts_b):
        cut = pl.ds(c * chunk, chunk)
        sent(saved.at[cut], ("MIRROR", c))
        sent(qs_b.at[c, seven], ("QB", c))
        sent(ks_b.at[c, seven], ("KB", c))
        sent(sr_b.at[c, seven], ("SB", c))
        sent(kv_b.at[c, seven], ("KVB", c))
    sent(wq.at[0], "WQ")
    for j in range(4):

        @pl.when(4 * d + j != t)
        def _():
            sent(wot.at[0], "WOT")

    @pl.when(home == d)
    def _():
        sent(wot, "FWD")

    sent(gr.at[0], "GRAD")
    for ref, name in (
        (qs_f, "QF"), (ks_f, "KF"), (sr_f, "SF"), (kv_f, "KVF"), (gms, "GM"), (mix_f, "MIXF"),
        (gks, "GK"), (gkv, "GKV"), (gq, "GQ"), (gq, "MIXB"),
    ):
        sent(ref.at[seven], name)

    @pl.when(home != d)
    def _():
        sent(mixb_own, "MIXB")

    sent(gq_sib, "GQS")
    sent(gkv_sib, "GKVS")
    sent(nb, "NB")
    sent(gn, "GN")

    @pl.when(s < n_pipe - 1)
    def _():
        sent(y, "NEXT")

    @pl.when(s > 0)
    def _():
        sent(gx, "PREV")

    for i in range(4):

        @pl.when(jnp.logical_not(jnp.logical_and(4 * d + i == t, home == d)))
        def _():
            sent(wog.at[i], "WOG")

    got(gwo_out, "WOG")
    got(next_out, "NEXT")
    got(prev_out, "PREV")


def place(*refs):
    count = len(refs) // 2
    sem = refs[-1]
    copies = [
        pltpu.make_async_copy(refs[i], refs[count + i], sem.at[i]) for i in range(count)
    ]
    for copy in copies:
        copy.start()
    for copy in copies:
        copy.wait()


def local(fwd_in, parked, grad_in, positions, kv_cache, w_query, w_keyval, w_out, gain):
    n_pipe = lax.axis_size("pipe")
    nt = lax.axis_size("tensor")
    rows, feat = fwd_in.shape[1:]
    span = kv_cache.shape[3]
    part = w_out.shape[2] // 4
    any_ = pl.BlockSpec(memory_space=pltpu.HBM)
    vmem = pl.BlockSpec(memory_space=pltpu.VMEM)

    def V(*shape, dtype=BF):
        return pltpu.VMEM(shape, dtype)

    parts_b = 2
    cut = rows // parts_b
    heads = (nt, rows, HEAD)
    heads_b = (parts_b, nt, cut, HEAD)
    strips = (nt, rows // nt, 2 * HEAD)
    strips_b = (parts_b, nt, cut // nt, 2 * HEAD)

    out = pl.pallas_call(
        functools.partial(kernel, n_pipe, feat * nt),
        out_shape=(
            pltpu.VMEM((rows, feat), BF),
            pltpu.VMEM((rows, feat), BF),
            pltpu.VMEM(w_query.shape[1:], BF),
            pltpu.VMEM(w_keyval.shape[1:], F32),
            pltpu.VMEM(w_out.shape[1:], BF),
            pltpu.VMEM((1, feat), F32),
        ),
        in_specs=[any_] * 9,
        out_specs=(vmem,) * 6,
        scratch_shapes=[
            V(rows, feat), V(rows, feat), V(2, rows, feat), V(2, span, 2 * HEAD),
            V(2, *w_query.shape[1:]), V(*w_keyval.shape[1:]), V(nt, HEAD, part),
            V(*heads), V(*heads), V(*heads_b), V(*heads_b),
            V(*strips), V(*strips), V(*strips_b), V(*strips_b),
            V(8, rows, dtype=F32), V(nt, 8, rows, dtype=F32),
            V(parts_b, 8, cut, dtype=F32), V(parts_b, nt, 8, cut, dtype=F32),
            V(*strips), V(*strips_b), V(rows, HEAD, dtype=F32), V(parts_b, cut, HEAD, dtype=F32),
            V(*heads), V(*heads), V(*heads), V(rows, HEAD), V(2, 4, rows, HEAD),
            V(*strips), V(*strips), V(*strips), V(*heads), V(4, rows, HEAD), V(*strips),
            V(rows, feat), V(rows, feat),
            V(rows, feat), V(rows, feat), V(rows, feat), V(4, HEAD, part),
            V(8, feat, dtype=F32), V(8, feat, dtype=F32),
            pltpu.SMEM((1, 2), jnp.int32), V(1, feat),
            pltpu.SemaphoreType.DMA((7,)),
            pltpu.SemaphoreType.DMA((8,)),
            pltpu.SemaphoreType.DMA((22 + 5 * parts_b,)),
            pltpu.SemaphoreType.DMA((22 + 5 * parts_b,)),
        ],
        compiler_params=pltpu.CompilerParams(
            collective_id=0, has_side_effects=True, vmem_limit_bytes=32 * 1024 * 1024
        ),
        name="relay",
    )(
        *(
            pltpu.with_memory_space_constraint(v, pltpu.HBM)
            for v in (
                positions[0], gain, fwd_in[0], parked[0], grad_in[0], kv_cache[0, 0], w_query[0], w_keyval[0], w_out[0]
            )
        ),
    )
    next_act, prev_grad, gwq, gwkv, gwo, ggain = pl.pallas_call(
        place,
        out_shape=tuple(jax.ShapeDtypeStruct(v.shape, v.dtype) for v in out),
        in_specs=[vmem] * len(out),
        out_specs=(any_,) * len(out),
        scratch_shapes=[pltpu.SemaphoreType.DMA((len(out),))],
        compiler_params=pltpu.CompilerParams(vmem_limit_bytes=4 * 1024 * 1024),
        name="place",
    )(*out)
    return next_act[None], prev_grad[None], gwq[None], gwkv[None], gwo[None], ggain


def solution(mesh):
    return jax.shard_map(
        local,
        mesh=mesh,
        in_specs=(
            P("pipe", "dp", "tensor"),
            P("pipe", "dp", "tensor"),
            P("pipe", "dp", "tensor"),
            P("pipe", "dp", None),
            P("pipe", "dp", None, None, None),
            P("pipe", "tensor", "dp"),
            P("pipe", "tensor", None),
            P("pipe", "tensor", "dp"),
            P("pipe", "tensor"),
        ),
        out_specs=(
            P("pipe", "dp", "tensor"),
            P("pipe", "dp", "tensor"),
            P("pipe", "tensor", "dp"),
            P("pipe", "tensor", None),
            P("pipe", "tensor", "dp"),
            P("pipe", "tensor"),
        ),
        check_vma=False,
    )
```
